32 devices in a mesh: groups: 2 (over y), aux: 4 (over z), basis: 2 (over x), occ: 2 (over core).
Axes of the slice: x: 2, y: 2, z: 4, core: 2. Of those that a mesh axis runs over, the one named last changes fastest.
Arguments:
- integrals: bfloat16 [4096, 8, 2048], P(('groups', 'basis'), 'aux', 'occ'), parts along dimension 0, may hold values from -0.5 to 0.5
- need_blocks: int32 [4, 8], P('groups'), parts along dimension 0, may hold values from 0 to 15, as said below
- pair_first: int32 [4, 24], P('groups'), parts along dimension 0, may hold values from 0 to 6, as said below
- pair_second: int32 [4, 24], P('groups'), parts along dimension 0, may hold values from 1 to 7
- pair_count: int32 [4], P('groups'), parts along dimension 0, may hold values from 8 to 24, as said below
Outputs:
- k_tiles: float32 [4, 24, 128, 128], P(('groups', 'basis'), None, ('aux', 'occ')), parts along dimension 0
The draws below stay inside these ranges and needn't reach their ends.
There are 2 independent parts, one for each index of `groups`. The reference program is written for one: setup_inputs(seed, part) draws one part's arguments, and reference() takes and returns one part's arrays. A program takes and returns all parts, laid end to end along the dimension named above; each array names one. Nothing has to cross between parts.
Inputs may be any that keep to these rules, and one draw needn't show every extreme that they name: `need_blocks`: each row lists 8 different blocks in rising order; at most 4 of a row lie in one index of basis's range (blocks b * 8 to (b + 1) * 8 - 1), and exactly 4 in some range in every row. pair_first[k, p] < pair_second[k, p]; the pairs of one owner are different. `pair_count`: some owner has exactly 24 live pairs.
All inputs are finite; a program needn't handle non-finite values.
Results may differ from the reference program's by a relative error of at most 0.0003.
Values may be sent and summed in bfloat16 or wider, within the bound.
A program may use at most 64 MiB of HBM per device.

```python
import jax
import jax.numpy as jnp
import numpy as np
from jax import lax

BLK = 128
OCC = 2048
BLK_DEV = 8
U = 8
PMAX = 24
AUX = 8
NBLK = 16
NOWN = 2
SRC_MOST = 4
N_BASIS = 2


def draw_need_blocks(key, part):
    key = jax.random.fold_in(key, 11)

    def one_owner(owner_key):
        sorting_key, block_key = jax.random.split(owner_key)
        order = jax.random.permutation(sorting_key, N_BASIS)
        order_rank = jnp.argsort(order)
        counts = jnp.clip(U - order_rank * SRC_MOST, 0, SRC_MOST)
        picks = jax.vmap(lambda inner: jax.random.permutation(inner, BLK_DEV)[:SRC_MOST])(jax.random.split(block_key, N_BASIS))
        block_ids = jnp.arange(N_BASIS)[:, None] * BLK_DEV + picks
        valid = jnp.arange(SRC_MOST)[None, :] < counts[:, None]
        scores = jnp.where(valid, block_ids, NBLK + 1).reshape(-1)
        return jnp.sort(scores)[:U].astype(jnp.int32)
    return jax.vmap(one_owner)(jax.random.split(key, NOWN))


def pair_table(key):
    firsts, seconds = np.triu_indices(U, 1)
    firsts = jnp.asarray(firsts, dtype=jnp.int32)
    seconds = jnp.asarray(seconds, dtype=jnp.int32)
    keys = jax.random.split(key, NOWN)
    combos = firsts.shape[0]
    chosen = jax.vmap(lambda inner: jax.random.permutation(inner, combos)[:PMAX])(keys)
    return (firsts[chosen], seconds[chosen])


def draw_pair_first(key, part):
    table = pair_table(key)
    return table[0]


def draw_pair_second(key, part):
    table = pair_table(key)
    return table[1]


def draw_pair_count(key, part):
    key = jax.random.fold_in(key, 14)
    count_key, busy_key = jax.random.split(key)
    counts = jax.random.randint(count_key, (NOWN,), PMAX // 3, PMAX + 1)
    busiest = jax.random.randint(busy_key, (), 0, NOWN)
    counts = jnp.where(jnp.arange(NOWN) == busiest, PMAX, counts)
    return counts.astype(jnp.int32)


def levels(own_key, dims, shards, low, top_value):
    def one(axis_at, parts):
        steps = jax.random.uniform(jax.random.fold_in(jax.random.fold_in(own_key, 6), axis_at), (parts,), jnp.float32, low / len(shards), top_value / len(shards))
        return jnp.repeat(jnp.exp(steps), dims[axis_at] // parts).reshape((-1,) + (1,) * (len(dims) - axis_at - 1))

    loudness = one(*shards[0])
    for cut in shards[1:]:
        loudness = loudness * one(*cut)
    return loudness


def gaussian(rng, extent, deviation, most, cuts=(), kind=jnp.bfloat16):
    gain = levels(rng, extent, cuts, -0.22, 0.18) if cuts else 1.0
    array = jax.random.normal(rng, extent, jnp.float32) * deviation * gain
    return jnp.minimum(jnp.maximum(array, -most), most).astype(kind)


def setup_inputs(seed: int = 0, part: int = 0) -> dict:
    seeds = jax.random.split(jax.random.key(seed), 6)
    own_keys = jax.random.split(jax.random.fold_in(seeds[5], part), 6)
    return {
        "integrals": gaussian(own_keys[0], (NBLK * BLK, AUX, OCC), ((AUX * OCC) ** -0.25), 0.5, ((0, 2), (1, 4), (2, 2))),
        "need_blocks": draw_need_blocks(jax.random.fold_in(jax.random.fold_in(seeds[5], part), 71), part),
        "pair_first": draw_pair_first(jax.random.fold_in(jax.random.fold_in(seeds[5], part), 71), part),
        "pair_second": draw_pair_second(jax.random.fold_in(jax.random.fold_in(seeds[5], part), 71), part),
        "pair_count": draw_pair_count(jax.random.fold_in(jax.random.fold_in(seeds[5], part), 71), part),
    }


def reference(integrals, need_blocks, pair_first, pair_second, pair_count):
    blocks = integrals.reshape(NBLK, BLK, AUX * OCC)

    def owner_tiles(owner_id):
        wanted = need_blocks[owner_id]

        def one_pair(slot):
            leading_block_index = wanted[pair_first[owner_id, slot]].astype(jnp.int32)
            second_block = wanted[pair_second[owner_id, slot]].astype(jnp.int32)
            bra_block_rows = lax.dynamic_index_in_dim(blocks, leading_block_index, 0, keepdims=False)
            ket_block_rows = lax.dynamic_index_in_dim(blocks, second_block, 0, keepdims=False)
            tile = jnp.dot(bra_block_rows, ket_block_rows.T, preferred_element_type=jnp.float32)
            return jnp.where(slot < pair_count[owner_id], tile, jnp.zeros_like(tile))

        return lax.map(one_pair, jnp.arange(PMAX, dtype=jnp.int32))

    return lax.map(owner_tiles, jnp.arange(NOWN, dtype=jnp.int32))
```

```python
import functools

import jax
import jax.numpy as jnp
from jax import lax
from jax.experimental import pallas as pl
from jax.experimental.pallas import tpu as pltpu
from jax.sharding import PartitionSpec as P

BLK = 128
MESH = pl.DeviceIdType.MESH


def kernel(
    nb, nz, nc, per,
    need_ref, first_ref, second_ref, count_ref, x_ref,
    out_ref,
    xv, sent, held, mine, part, other, summed, come, total,
    load_sem, x_send, x_recv, c_send, c_recv, z_send, z_recv,
):
    b = lax.axis_index("basis")
    z = lax.axis_index("aux")
    c = lax.axis_index("occ")
    local = xv.shape[0]
    rows = part.shape[3]
    pmax = out_ref.shape[0]

    loads = []
    for i in range(local):
        load = pltpu.make_async_copy(x_ref.at[i], xv.at[i], load_sem.at[i])
        load.start()
        loads.append(load)

    x_peers = [lax.rem(b + s, nb) for s in range(1, nb)]
    z_peers = [lax.rem(z + o, nz) for o in range(1, nz)]
    c_peers = [lax.rem(c + o, nc) for o in range(1, nc)]
    barrier = pltpu.get_barrier_semaphore()
    for d in x_peers:
        pl.semaphore_signal(barrier, inc=1, device_id={"basis": d}, device_id_type=MESH)
    for d in z_peers:
        pl.semaphore_signal(barrier, inc=1, device_id={"aux": d}, device_id_type=MESH)
    for d in c_peers:
        pl.semaphore_signal(barrier, inc=1, device_id={"occ": d}, device_id_type=MESH)
    for load in loads:
        load.wait()
    pl.semaphore_wait(barrier, len(x_peers) + len(z_peers) + len(c_peers))

    def pack(owner, j, dst):
        block = lax.rem(need_ref[owner, b * per + j], local)

        def rows_of(r, _):
            at = pl.ds(pl.multiple_of(r * 32, 32), 32)
            dst[at, :] = xv[block, at, :]
            return 0

        lax.fori_loop(0, BLK // 32, rows_of, 0)

    pending = []
    for s in range(1, nb):
        d = lax.rem(b + nb - s, nb)
        for j in range(per):
            k = (s - 1) * per + j
            pack(d, j, sent.at[k])
            copy = pltpu.make_async_remote_copy(
                src_ref=sent.at[k],
                dst_ref=held.at[k],
                send_sem=x_send.at[k],
                recv_sem=x_recv.at[k],
                device_id={"basis": d},
                device_id_type=MESH,
            )
            copy.start()
            pending.append(copy)
    for j in range(per):
        pack(b, j, mine.at[j])

    def put(tile, slot):
        for q in range(nz * nc):
            part[q % nc, q // nc, slot] = tile[q * rows:(q + 1) * rows, :]

    def product(lhs, rhs):
        return lax.dot_general(
            lhs, rhs, (((1,), (1,)), ((), ())), preferred_element_type=jnp.float32
        )

    def exchange(step, lo, hi):
        copies = []
        for o, d in enumerate(c_peers):
            copy = pltpu.make_async_remote_copy(
                src_ref=part.at[d, :, lo:hi],
                dst_ref=other.at[o, :, lo:hi],
                send_sem=c_send.at[step, o],
                recv_sem=c_recv.at[step, o],
                device_id={"occ": d},
                device_id_type=MESH,
            )
            copy.start()
            copies.append(copy)
        return copies

    def spread(step, lo, hi):
        for slot in range(lo, hi):
            for q in range(nz):
                value = part[c, q, slot]
                for o in range(len(c_peers)):
                    value = value + other[o, q, slot]
                summed[q, slot] = value
        copies = []
        for o, d in enumerate(z_peers):
            copy = pltpu.make_async_remote_copy(
                src_ref=summed.at[d, lo:hi],
                dst_ref=come.at[o, lo:hi],
                send_sem=z_send.at[step, o],
                recv_sem=z_recv.at[step, o],
                device_id={"aux": d},
                device_id_type=MESH,
            )
            copy.start()
            copies.append(copy)
        return copies

    def finish(copies, lo, hi):
        for copy in copies:
            copy.wait()
        for slot in range(lo, hi):
            value = summed[z, slot]
            for o in range(len(z_peers)):
                value = value + come[o, slot]
            total[slot] = value

    def reduce(step, lo, hi):
        copies = exchange(step, lo, hi)
        for copy in copies:
            copy.wait()
        return spread(step, lo, hi)

    for a in range(1, per):
        for e in range(a):
            put(product(mine[e], mine[a]), a * (a - 1) // 2 + e)
    waiting = None
    lo, hi = 0, per * (per - 1) // 2
    waiting = (reduce(0, lo, hi), lo, hi)
    for a in range(per, nb * per):
        k = a - per
        s = a // per
        wrap = (b + s) // nb
        pending[k].wait_recv()
        base = a * (a - 1) // 2

        @pl.when(wrap == 0)
        def _():
            for e in range(per):
                put(product(mine[e], held[k]), base + e)

        @pl.when(wrap != 0)
        def _():
            for e in range(per):
                put(product(held[k], mine[e]), base + e)

        for e in range(per, a):
            flip = wrap - (b + e // per) // nb
            first = (e - per) + flip * (a - e)
            second = k - flip * (a - e)
            put(product(held[first], held[second]), base + e)
        lo, hi = base, base + a
        moving = reduce(a - per + 1, lo, hi)
        finish(*waiting)
        waiting = (moving, lo, hi)
    finish(*waiting)
    for copy in pending:
        copy.wait_send()

    live = count_ref[b]
    for p in range(pmax):
        u = first_ref[b, p]
        v = second_ref[b, p]
        u = lax.rem(u // per - b + nb, nb) * per + lax.rem(u, per)
        v = lax.rem(v // per - b + nb, nb) * per + lax.rem(v, per)
        big = jnp.maximum(u, v)
        small = jnp.minimum(u, v)
        value = total[jnp.minimum(big * (big - 1) // 2 + small, total.shape[0] - 1)]
        out_ref[p] = jnp.where(p < live, value, jnp.zeros_like(value))


def shards(mesh, integrals, need_blocks, pair_first, pair_second, pair_count):
    nb, nz, nc = mesh.shape["basis"], mesh.shape["aux"], mesh.shape["occ"]
    size, aux_size, occ_size = integrals.shape
    local = size // BLK
    width = aux_size * occ_size
    pmax = pair_first.shape[1]
    blocks = need_blocks.shape[1]
    per = blocks // nb
    slots = blocks * (blocks - 1) // 2
    rows = BLK // (nz * nc)
    steps = 1 + blocks - per
    x = integrals.reshape(local, BLK, width)
    f32, bf16 = jnp.float32, jnp.bfloat16
    out = pl.pallas_call(
        functools.partial(kernel, nb, nz, nc, per),
        out_shape=jax.ShapeDtypeStruct((pmax, rows, BLK), f32),
        in_specs=[pl.BlockSpec(memory_space=pltpu.SMEM)] * 4 + [pl.BlockSpec(memory_space=pl.ANY)],
        out_specs=pl.BlockSpec(memory_space=pltpu.VMEM),
        scratch_shapes=[
            pltpu.VMEM((local, BLK, width), bf16),
            pltpu.VMEM((blocks - per, BLK, width), bf16),
            pltpu.VMEM((blocks - per, BLK, width), bf16),
            pltpu.VMEM((per, BLK, width), bf16),
            pltpu.VMEM((nc, nz, slots, rows, BLK), f32),
            pltpu.VMEM((nc - 1, nz, slots, rows, BLK), f32),
            pltpu.VMEM((nz, slots, rows, BLK), f32),
            pltpu.VMEM((nz - 1, slots, rows, BLK), f32),
            pltpu.VMEM((slots, rows, BLK), f32),
            pltpu.SemaphoreType.DMA((local,)),
            pltpu.SemaphoreType.DMA((blocks - per,)),
            pltpu.SemaphoreType.DMA((blocks - per,)),
            pltpu.SemaphoreType.DMA((steps, nc - 1)),
            pltpu.SemaphoreType.DMA((steps, nc - 1)),
            pltpu.SemaphoreType.DMA((steps, nz - 1)),
            pltpu.SemaphoreType.DMA((steps, nz - 1)),
        ],
        compiler_params=pltpu.CompilerParams(
            collective_id=0, has_side_effects=True, vmem_limit_bytes=48 * 2**20
        ),
    )(need_blocks, pair_first, pair_second, pair_count, x)
    return out[None]


def solution(mesh):
    in_specs = (
        P(("groups", "basis"), "aux", "occ"),
        P("groups", None),
        P("groups", None),
        P("groups", None),
        P("groups"),
    )
    out_specs = P(("groups", "basis"), None, ("aux", "occ"), None)
    return jax.shard_map(
        functools.partial(shards, mesh), mesh=mesh, in_specs=in_specs, out_specs=out_specs, check_vma=False
    )
```

```python
import functools

import jax
import jax.numpy as jnp
from jax import lax
from jax.experimental import pallas as pl
from jax.experimental.pallas import tpu as pltpu
from jax.sharding import PartitionSpec as P

BLK = 128
CUT = 4
MESH = pl.DeviceIdType.MESH


def kernel(
    nb, nz, nc, per,
    need_ref, first_ref, second_ref, count_ref, x_ref,
    out_ref,
    xv, sent, held, mine, part, other, summed, come, total,
    load_sem, x_send, x_recv, c_send, c_recv, z_send, z_recv,
):
    b = lax.axis_index("basis")
    z = lax.axis_index("aux")
    c = lax.axis_index("occ")
    local = xv.shape[0]
    rows = part.shape[3]
    pmax = out_ref.shape[0]

    loads = []
    for i in range(local):
        load = pltpu.make_async_copy(x_ref.at[i], xv.at[i], load_sem.at[i])
        load.start()
        loads.append(load)

    x_peers = [lax.rem(b + s, nb) for s in range(1, nb)]
    z_peers = [lax.rem(z + o, nz) for o in range(1, nz)]
    c_peers = [lax.rem(c + o, nc) for o in range(1, nc)]
    barrier = pltpu.get_barrier_semaphore()
    for d in x_peers:
        pl.semaphore_signal(barrier, inc=1, device_id={"basis": d}, device_id_type=MESH)
    for d in z_peers:
        pl.semaphore_signal(barrier, inc=1, device_id={"aux": d}, device_id_type=MESH)
    for d in c_peers:
        pl.semaphore_signal(barrier, inc=1, device_id={"occ": d}, device_id_type=MESH)
    for load in loads:
        load.wait()
    pl.semaphore_wait(barrier, len(x_peers) + len(z_peers) + len(c_peers))

    def pack(owner, j, dst):
        block = lax.rem(need_ref[owner, b * per + j], local)

        def rows_of(r, _):
            at = pl.ds(pl.multiple_of(r * 32, 32), 32)
            dst[at, :] = xv[block, at].reshape(32, dst.shape[1])
            return 0

        lax.fori_loop(0, BLK // 32, rows_of, 0)

    pending = []
    piece = BLK // CUT
    for s in range(1, nb):
        d = lax.rem(b + nb - s, nb)
        for j in range(per):
            k = (s - 1) * per + j
            pack(d, j, sent.at[k])
            for i in range(CUT):
                at = pl.ds(i * piece, piece)
                copy = pltpu.make_async_remote_copy(
                    src_ref=sent.at[k, at],
                    dst_ref=held.at[k, at],
                    send_sem=x_send.at[k, i],
                    recv_sem=x_recv.at[k, i],
                    device_id={"basis": d},
                    device_id_type=MESH,
                )
                pending.append(copy)
                if len(pending) <= CUT:
                    copy.start()
    for j in range(per):
        pack(b, j, mine.at[pl.ds(j * BLK, BLK)])

    def put(tile, slot):
        for q in range(nz * nc):
            part[q % nc, q // nc, slot] = tile[q * rows:(q + 1) * rows, :]

    def product(lhs, rhs):
        return lax.dot_general(
            lhs, rhs, (((1,), (1,)), ((), ())), preferred_element_type=jnp.float32
        )

    def exchange(step, lo, hi):
        copies = []
        for o, d in enumerate(c_peers):
            copy = pltpu.make_async_remote_copy(
                src_ref=part.at[d, :, lo:hi],
                dst_ref=other.at[o, :, lo:hi],
                send_sem=c_send.at[step, o],
                recv_sem=c_recv.at[step, o],
                device_id={"occ": d},
                device_id_type=MESH,
            )
            copy.start()
            copies.append(copy)
        return copies

    def spread(step, lo, hi):
        for slot in range(lo, hi):
            for q in range(nz):
                value = part[c, q, slot]
                for o in range(len(c_peers)):
                    value = value + other[o, q, slot]
                summed[q, slot] = value
        copies = []
        for o, d in enumerate(z_peers):
            copy = pltpu.make_async_remote_copy(
                src_ref=summed.at[d, lo:hi],
                dst_ref=come.at[o, lo:hi],
                send_sem=z_send.at[step, o],
                recv_sem=z_recv.at[step, o],
                device_id={"aux": d},
                device_id_type=MESH,
            )
            copy.start()
            copies.append(copy)
        return copies

    def finish(copies, lo, hi):
        for copy in copies:
            copy.wait()
        for slot in range(lo, hi):
            value = summed[z, slot]
            for o in range(len(z_peers)):
                value = value + come[o, slot]
            total[slot] = value

    def reduce(step, lo, hi):
        copies = exchange(step, lo, hi)
        for copy in copies:
            copy.wait()
        return spread(step, lo, hi)

    def own(j):
        return mine[j * BLK:(j + 1) * BLK, :]

    for a in range(1, per):
        for e in range(a):
            put(product(own(e), own(a)), a * (a - 1) // 2 + e)
    waiting = None
    lo, hi = 0, per * (per - 1) // 2
    waiting = (reduce(0, lo, hi), lo, hi)
    for a in range(per, nb * per):
        k = a - per
        s = a // per
        wrap = (b + s) // nb
        for i in range(k * CUT, (k + 1) * CUT):
            pending[i].wait_recv()
            if i + CUT < len(pending):
                pending[i + CUT].start()
        base = a * (a - 1) // 2

        @pl.when(wrap == 0)
        def _():
            wide = product(mine[...], held[k])
            for e in range(per):
                put(wide[e * BLK:(e + 1) * BLK, :], base + e)

        @pl.when(wrap != 0)
        def _():
            wide = product(held[k], mine[...])
            for e in range(per):
                put(wide[:, e * BLK:(e + 1) * BLK], base + e)

        for e in range(per, a):
            flip = wrap - (b + e // per) // nb
            first = (e - per) + flip * (a - e)
            second = k - flip * (a - e)
            put(product(held[first], held[second]), base + e)
        lo, hi = base, base + a
        moving = reduce(a - per + 1, lo, hi)
        finish(*waiting)
        waiting = (moving, lo, hi)
    finish(*waiting)
    for copy in pending:
        copy.wait_send()

    live = count_ref[b]
    for p in range(pmax):
        u = first_ref[b, p]
        v = second_ref[b, p]
        u = lax.rem(u // per - b + nb, nb) * per + lax.rem(u, per)
        v = lax.rem(v // per - b + nb, nb) * per + lax.rem(v, per)
        big = jnp.maximum(u, v)
        small = jnp.minimum(u, v)
        value = total[jnp.minimum(big * (big - 1) // 2 + small, total.shape[0] - 1)]
        out_ref[p] = jnp.where(p < live, value, jnp.zeros_like(value))


def shards(mesh, integrals, need_blocks, pair_first, pair_second, pair_count):
    nb, nz, nc = mesh.shape["basis"], mesh.shape["aux"], mesh.shape["occ"]
    size, aux_size, occ_size = integrals.shape
    local = size // BLK
    width = aux_size * occ_size
    pmax = pair_first.shape[1]
    blocks = need_blocks.shape[1]
    per = blocks // nb
    slots = blocks * (blocks - 1) // 2
    rows = BLK // (nz * nc)
    steps = 1 + blocks - per
    x = integrals.reshape(local, BLK, aux_size, occ_size)
    f32, bf16 = jnp.float32, jnp.bfloat16
    out = pl.pallas_call(
        functools.partial(kernel, nb, nz, nc, per),
        out_shape=jax.ShapeDtypeStruct((pmax, rows, BLK), f32),
        in_specs=[pl.BlockSpec(memory_space=pltpu.SMEM)] * 4 + [pl.BlockSpec(memory_space=pltpu.HBM)],
        out_specs=pl.BlockSpec(memory_space=pltpu.VMEM),
        scratch_shapes=[
            pltpu.VMEM((local, BLK, aux_size, occ_size), bf16),
            pltpu.VMEM((blocks - per, BLK, width), bf16),
            pltpu.VMEM((blocks - per, BLK, width), bf16),
            pltpu.VMEM((per * BLK, width), bf16),
            pltpu.VMEM((nc, nz, slots, rows, BLK), f32),
            pltpu.VMEM((nc - 1, nz, slots, rows, BLK), f32),
            pltpu.VMEM((nz, slots, rows, BLK), f32),
            pltpu.VMEM((nz - 1, slots, rows, BLK), f32),
            pltpu.VMEM((slots, rows, BLK), f32),
            pltpu.SemaphoreType.DMA((local,)),
            pltpu.SemaphoreType.DMA((blocks - per, CUT)),
            pltpu.SemaphoreType.DMA((blocks - per, CUT)),
            pltpu.SemaphoreType.DMA((steps, nc - 1)),
            pltpu.SemaphoreType.DMA((steps, nc - 1)),
            pltpu.SemaphoreType.DMA((steps, nz - 1)),
            pltpu.SemaphoreType.DMA((steps, nz - 1)),
        ],
        compiler_params=pltpu.CompilerParams(
            collective_id=0, has_side_effects=True, vmem_limit_bytes=61 * 2**20
        ),
    )(need_blocks, pair_first, pair_second, pair_count, x)
    return out[None]


def solution(mesh):
    in_specs = (
        P(("groups", "basis"), "aux", "occ"),
        P("groups", None),
        P("groups", None),
        P("groups", None),
        P("groups"),
    )
    out_specs = P(("groups", "basis"), None, ("aux", "occ"), None)
    return jax.shard_map(
        functools.partial(shards, mesh), mesh=mesh, in_specs=in_specs, out_specs=out_specs, check_vma=False
    )
```

```python
import functools

import jax
import jax.numpy as jnp
from jax import lax
from jax.experimental import pallas as pl
from jax.experimental.pallas import tpu as pltpu
from jax.sharding import PartitionSpec as P

BLK = 128
CUT = 4
MESH = pl.DeviceIdType.MESH


def kernel(
    nb, nz, nc, per,
    need_in, first_in, second_in, count_in, x_ref,
    out_ref,
    need_ref, first_ref, second_ref, count_ref, *rest,
):
    xv, rest = rest[:CUT], rest[CUT:]
    sent, held, mine, part, other, summed, come, total = rest[:8]
    load_sem, arg_sem, x_send, x_recv, c_send, c_recv, z_send, z_recv = rest[8:]
    b = lax.axis_index("basis")
    z = lax.axis_index("aux")
    c = lax.axis_index("occ")
    local = x_ref.shape[0]
    piece = BLK // CUT
    rows = part.shape[3]
    pmax = out_ref.shape[0]

    tables = []
    for i, (src, dst) in enumerate((
        (need_in, need_ref), (first_in, first_ref), (second_in, second_ref), (count_in, count_ref)
    )):
        table = pltpu.make_async_copy(src, dst, arg_sem.at[i])
        table.start()
        tables.append(table)
    loads = []
    for i in range(CUT):
        load = pltpu.make_async_copy(x_ref.at[:, pl.ds(i * piece, piece)], xv[i], load_sem.at[i])
        load.start()
        loads.append(load)

    x_peers = [lax.rem(b + s, nb) for s in range(1, nb)]
    z_peers = [lax.rem(z + o, nz) for o in range(1, nz)]
    c_peers = [lax.rem(c + o, nc) for o in range(1, nc)]
    barrier = pltpu.get_barrier_semaphore()
    for d in x_peers:
        pl.semaphore_signal(barrier, inc=1, device_id={"basis": d}, device_id_type=MESH)
    for d in z_peers:
        pl.semaphore_signal(barrier, inc=1, device_id={"aux": d}, device_id_type=MESH)
    for d in c_peers:
        pl.semaphore_signal(barrier, inc=1, device_id={"occ": d}, device_id_type=MESH)
    tables[0].wait()
    pl.semaphore_wait(barrier, len(x_peers) + len(z_peers) + len(c_peers))

    def pack(owner, j, i, dst):
        block = lax.rem(need_ref[owner, b * per + j], local)
        dst[...] = xv[i][block].reshape(piece, dst.shape[1])

    pending = []
    for s in range(1, nb):
        d = lax.rem(b + nb - s, nb)
        for j in range(per):
            k = (s - 1) * per + j
            for i in range(CUT):
                at = pl.ds(i * piece, piece)
                if len(pending) < CUT:
                    loads[i].wait()
                pack(d, j, i, sent.at[k, at])
                copy = pltpu.make_async_remote_copy(
                    src_ref=sent.at[k, at],
                    dst_ref=held.at[k, at],
                    send_sem=x_send.at[k, i],
                    recv_sem=x_recv.at[k, i],
                    device_id={"basis": d},
                    device_id_type=MESH,
                )
                pending.append(copy)
                if len(pending) <= CUT:
                    copy.start()
    for j in range(per):
        for i in range(CUT):
            pack(b, j, i, mine.at[pl.ds(j * BLK + i * piece, piece)])

    def put(tile, slot):
        for q in range(nz * nc):
            part[q % nc, q // nc, slot] = tile[q * rows:(q + 1) * rows, :]

    def product(lhs, rhs):
        return lax.dot_general(
            lhs, rhs, (((1,), (1,)), ((), ())), preferred_element_type=jnp.float32
        )

    def exchange(step, lo, hi):
        copies = []
        for o, d in enumerate(c_peers):
            copy = pltpu.make_async_remote_copy(
                src_ref=part.at[d, :, lo:hi],
                dst_ref=other.at[o, :, lo:hi],
                send_sem=c_send.at[step, o],
                recv_sem=c_recv.at[step, o],
                device_id={"occ": d},
                device_id_type=MESH,
            )
            copy.start()
            copies.append(copy)
        return copies

    def spread(step, lo, hi):
        for slot in range(lo, hi):
            for q in range(nz):
                value = part[c, q, slot]
                for o in range(len(c_peers)):
                    value = value + other[o, q, slot]
                summed[q, slot] = value
        copies = []
        for o, d in enumerate(z_peers):
            copy = pltpu.make_async_remote_copy(
                src_ref=summed.at[d, lo:hi],
                dst_ref=come.at[o, lo:hi],
                send_sem=z_send.at[step, o],
                recv_sem=z_recv.at[step, o],
                device_id={"aux": d},
                device_id_type=MESH,
            )
            copy.start()
            copies.append(copy)
        return copies

    def finish(copies, lo, hi):
        for copy in copies:
            copy.wait()
        for slot in range(lo, hi):
            value = summed[z, slot]
            for o in range(len(z_peers)):
                value = value + come[o, slot]
            total[slot] = value

    def reduce(step, lo, hi):
        copies = exchange(step, lo, hi)
        for copy in copies:
            copy.wait()
        return spread(step, lo, hi)

    def own(j):
        return mine[j * BLK:(j + 1) * BLK, :]

    for a in range(1, per):
        for e in range(a):
            put(product(own(e), own(a)), a * (a - 1) // 2 + e)
    waiting = None
    lo, hi = 0, per * (per - 1) // 2
    waiting = (reduce(0, lo, hi), lo, hi)
    for a in range(per, nb * per):
        k = a - per
        s = a // per
        wrap = (b + s) // nb
        for i in range(k * CUT, (k + 1) * CUT):
            pending[i].wait_recv()
            if i + CUT < len(pending):
                pending[i + CUT].start()
        base = a * (a - 1) // 2

        @pl.when(wrap == 0)
        def _():
            wide = product(mine[...], held[k])
            for e in range(per):
                put(wide[e * BLK:(e + 1) * BLK, :], base + e)

        @pl.when(wrap != 0)
        def _():
            wide = product(held[k], mine[...])
            for e in range(per):
                put(wide[:, e * BLK:(e + 1) * BLK], base + e)

        for e in range(per, a):
            flip = wrap - (b + e // per) // nb
            first = (e - per) + flip * (a - e)
            second = k - flip * (a - e)
            put(product(held[first], held[second]), base + e)
        lo, hi = base, base + a
        moving = reduce(a - per + 1, lo, hi)
        finish(*waiting)
        waiting = (moving, lo, hi)
    finish(*waiting)
    for copy in pending:
        copy.wait_send()

    for table in tables[1:]:
        table.wait()
    live = count_ref[b]
    for p in range(pmax):
        u = first_ref[b, p]
        v = second_ref[b, p]
        u = lax.rem(u // per - b + nb, nb) * per + lax.rem(u, per)
        v = lax.rem(v // per - b + nb, nb) * per + lax.rem(v, per)
        big = jnp.maximum(u, v)
        small = jnp.minimum(u, v)
        value = total[jnp.minimum(big * (big - 1) // 2 + small, total.shape[0] - 1)]
        out_ref[p] = jnp.where(p < live, value, jnp.zeros_like(value))


def shards(mesh, integrals, need_blocks, pair_first, pair_second, pair_count):
    nb, nz, nc = mesh.shape["basis"], mesh.shape["aux"], mesh.shape["occ"]
    size, aux_size, occ_size = integrals.shape
    local = size // BLK
    width = aux_size * occ_size
    pmax = pair_first.shape[1]
    blocks = need_blocks.shape[1]
    per = blocks // nb
    slots = blocks * (blocks - 1) // 2
    rows = BLK // (nz * nc)
    steps = 1 + blocks - per
    x = integrals.reshape(local, BLK, aux_size, occ_size)
    f32, bf16 = jnp.float32, jnp.bfloat16
    out = pl.pallas_call(
        functools.partial(kernel, nb, nz, nc, per),
        out_shape=jax.ShapeDtypeStruct((pmax, rows, BLK), f32),
        in_specs=[pl.BlockSpec(memory_space=pltpu.HBM)] * 5,
        out_specs=pl.BlockSpec(memory_space=pltpu.VMEM),
        scratch_shapes=[
            *[
                pltpu.SMEM(table.shape, jnp.int32)
                for table in (need_blocks, pair_first, pair_second, pair_count)
            ],
            *[pltpu.VMEM((local, BLK // CUT, aux_size, occ_size), bf16)] * CUT,
            pltpu.VMEM((blocks - per, BLK, width), bf16),
            pltpu.VMEM((blocks - per, BLK, width), bf16),
            pltpu.VMEM((per * BLK, width), bf16),
            pltpu.VMEM((nc, nz, slots, rows, BLK), f32),
            pltpu.VMEM((nc - 1, nz, slots, rows, BLK), f32),
            pltpu.VMEM((nz, slots, rows, BLK), f32),
            pltpu.VMEM((nz - 1, slots, rows, BLK), f32),
            pltpu.VMEM((slots, rows, BLK), f32),
            pltpu.SemaphoreType.DMA((CUT,)),
            pltpu.SemaphoreType.DMA((4,)),
            pltpu.SemaphoreType.DMA((blocks - per, CUT)),
            pltpu.SemaphoreType.DMA((blocks - per, CUT)),
            pltpu.SemaphoreType.DMA((steps, nc - 1)),
            pltpu.SemaphoreType.DMA((steps, nc - 1)),
            pltpu.SemaphoreType.DMA((steps, nz - 1)),
            pltpu.SemaphoreType.DMA((steps, nz - 1)),
        ],
        compiler_params=pltpu.CompilerParams(
            collective_id=0, has_side_effects=True, vmem_limit_bytes=61 * 2**20
        ),
    )(need_blocks, pair_first, pair_second, pair_count, x)
    return out[None]


def solution(mesh):
    in_specs = (
        P(("groups", "basis"), "aux", "occ"),
        P("groups", None),
        P("groups", None),
        P("groups", None),
        P("groups"),
    )
    out_specs = P(("groups", "basis"), None, ("aux", "occ"), None)
    return jax.shard_map(
        functools.partial(shards, mesh), mesh=mesh, in_specs=in_specs, out_specs=out_specs, check_vma=False
    )
```

```python
import functools

import jax
import jax.numpy as jnp
from jax import lax
from jax.experimental import pallas as pl
from jax.experimental.pallas import tpu as pltpu
from jax.sharding import PartitionSpec as P

BLK = 128
CUT = 4
MESH = pl.DeviceIdType.MESH


def kernel(
    nb, nz, nc, per, split,
    need_in, first_in, second_in, count_in, x_ref,
    out_ref,
    need_ref, first_ref, second_ref, count_ref, *rest,
):
    xv, rest = rest[:CUT], rest[CUT:]
    sent, held, mine, part, other, summed, come, total, spare = rest[:9]
    load_sem, arg_sem, x_send, x_recv, c_send, c_recv, z_send, z_recv, g_send, g_recv = rest[9:]
    b = lax.axis_index("basis")
    z = lax.axis_index("aux")
    c = lax.axis_index("occ")
    local = x_ref.shape[0]
    piece = BLK // CUT
    rows = part.shape[3]
    pmax = out_ref.shape[0]

    tables = []
    for i, (src, dst) in enumerate((
        (need_in, need_ref), (first_in, first_ref), (second_in, second_ref), (count_in, count_ref)
    )):
        table = pltpu.make_async_copy(src, dst, arg_sem.at[i])
        table.start()
        tables.append(table)
    loads = []
    for i in range(CUT):
        load = pltpu.make_async_copy(x_ref.at[:, pl.ds(i * piece, piece)], xv[i], load_sem.at[i])
        load.start()
        loads.append(load)

    x_peers = [lax.rem(b + s, nb) for s in range(1, nb)]
    z_peers = [lax.rem(z + o, nz) for o in range(1, nz)]
    c_peers = [lax.rem(c + o, nc) for o in range(1, nc)]
    barrier = pltpu.get_barrier_semaphore()
    for d in x_peers:
        pl.semaphore_signal(barrier, inc=1, device_id={"basis": d}, device_id_type=MESH)
    for d in z_peers:
        pl.semaphore_signal(barrier, inc=1, device_id={"aux": d}, device_id_type=MESH)
    for d in c_peers:
        pl.semaphore_signal(barrier, inc=1, device_id={"occ": d}, device_id_type=MESH)
    tables[0].wait()
    pl.semaphore_wait(barrier, len(x_peers) + len(z_peers) + len(c_peers))

    def pack(owner, j, i, dst):
        block = lax.rem(need_ref[owner, b * per + j], local)
        dst[...] = xv[i][block].reshape(piece, dst.shape[1])

    def pack_strided(owner, j, i, dst):
        block = lax.rem(need_ref[owner, b * per + j], local)
        h, quarter = i // 2, i % 2
        taken = []
        for n in range(4):
            row = 16 * (4 * quarter + n) + 8 * h
            taken.append(xv[row // piece][block, row % piece:row % piece + 8])
        dst[...] = jnp.concatenate(taken, axis=0).reshape(piece, dst.shape[1])

    pending = []
    for s in range(1, nb):
        d = lax.rem(b + nb - s, nb)
        for j in range(per):
            k = (s - 1) * per + j
            for i in range(CUT):
                at = pl.ds(i * piece, piece)
                if len(pending) < CUT:
                    loads[i].wait()
                if split and k == per - 1:
                    @pl.when(d == 0)
                    def _():
                        pack(d, j, i, sent.at[k, at])

                    @pl.when(d != 0)
                    def _():
                        pack_strided(d, j, i, sent.at[k, at])

                    pack(d, j, i, spare.at[at])
                else:
                    pack(d, j, i, sent.at[k, at])
                copy = pltpu.make_async_remote_copy(
                    src_ref=sent.at[k, at],
                    dst_ref=held.at[k, at],
                    send_sem=x_send.at[k, i],
                    recv_sem=x_recv.at[k, i],
                    device_id={"basis": d},
                    device_id_type=MESH,
                )
                pending.append(copy)
                if len(pending) <= CUT:
                    copy.start()
    for j in range(per):
        for i in range(CUT):
            pack(b, j, i, mine.at[pl.ds(j * BLK + i * piece, piece)])

    def put(tile, slot):
        for q in range(nz * nc):
            part[q % nc, q // nc, slot] = tile[q * rows:(q + 1) * rows, :]

    def product(lhs, rhs):
        return lax.dot_general(
            lhs, rhs, (((1,), (1,)), ((), ())), preferred_element_type=jnp.float32
        )

    def exchange(step, lo, hi):
        copies = []
        for o, d in enumerate(c_peers):
            copy = pltpu.make_async_remote_copy(
                src_ref=part.at[d, :, lo:hi],
                dst_ref=other.at[o, :, lo:hi],
                send_sem=c_send.at[step, o],
                recv_sem=c_recv.at[step, o],
                device_id={"occ": d},
                device_id_type=MESH,
            )
            copy.start()
            copies.append(copy)
        return copies

    def spread(step, lo, hi):
        for slot in range(lo, hi):
            for q in range(nz):
                value = part[c, q, slot]
                for o in range(len(c_peers)):
                    value = value + other[o, q, slot]
                summed[q, slot] = value
        copies = []
        for o, d in enumerate(z_peers):
            copy = pltpu.make_async_remote_copy(
                src_ref=summed.at[d, lo:hi],
                dst_ref=come.at[o, lo:hi],
                send_sem=z_send.at[step, o],
                recv_sem=z_recv.at[step, o],
                device_id={"aux": d},
                device_id_type=MESH,
            )
            copy.start()
            copies.append(copy)
        return copies

    def finish(copies, lo, hi):
        for copy in copies:
            copy.wait()
        for slot in range(lo, hi):
            value = summed[z, slot]
            for o in range(len(z_peers)):
                value = value + come[o, slot]
            total[slot] = value

    def reduce(step, lo, hi):
        copies = exchange(step, lo, hi)
        for copy in copies:
            copy.wait()
        return spread(step, lo, hi)

    def own(j):
        return mine[j * BLK:(j + 1) * BLK, :]

    for a in range(1, per):
        for e in range(a):
            put(product(own(e), own(a)), a * (a - 1) // 2 + e)
    lo, hi = 0, per * (per - 1) // 2
    waiting = [(reduce(0, lo, hi), lo, hi)]
    step = 1
    give = None
    if split:
        base = total.shape[0] - (per - 1)
        for e in range(per - 1):
            put(product(sent[e], spare[...]), base + e)
        waiting.append((reduce(step, base, base + per - 1), base, base + per - 1))
        step += 1
        give = pltpu.make_async_remote_copy(
            src_ref=total.at[base:base + per - 1],
            dst_ref=total.at[base - (per - 1):base],
            send_sem=g_send,
            recv_sem=g_recv,
            device_id={"basis": x_peers[0]},
            device_id_type=MESH,
        )
    for a in range(per, nb * per):
        k = a - per
        s = a // per
        wrap = (b + s) // nb
        base = a * (a - 1) // 2
        if split and a == nb * per - 1:
            break
        for i in range(k * CUT, (k + 1) * CUT):
            pending[i].wait_recv()
            if i + CUT < len(pending):
                pending[i + CUT].start()

        @pl.when(wrap == 0)
        def _():
            wide = product(mine[...], held[k])
            for e in range(per):
                put(wide[e * BLK:(e + 1) * BLK, :], base + e)

        @pl.when(wrap != 0)
        def _():
            wide = product(held[k], mine[...])
            for e in range(per):
                put(wide[:, e * BLK:(e + 1) * BLK], base + e)

        for e in range(per, a):
            flip = wrap - (b + e // per) // nb
            first = (e - per) + flip * (a - e)
            second = k - flip * (a - e)
            put(product(held[first], held[second]), base + e)
        lo, hi = base, base + a
        moving = reduce(step, lo, hi)
        step += 1
        for move in waiting:
            finish(*move)
        waiting = [(moving, lo, hi)]
        if split and a == per:
            give.start()
    if split:
        half = BLK // 2
        for h in range(2):
            for i in range(k * CUT + 2 * h, k * CUT + 2 * h + 2):
                pending[i].wait_recv()
            at = slice(h * half, (h + 1) * half)

            @pl.when(wrap == 0)
            def _():
                wide = product(mine[...], held[k, at])
                for m in range(per // 2):
                    left = wide[2 * m * BLK:(2 * m + 1) * BLK, :]
                    right = wide[(2 * m + 1) * BLK:(2 * m + 2) * BLK, :]
                    put(jnp.concatenate([left, right], axis=1), base + h * per // 2 + m)

            @pl.when(wrap != 0)
            def _():
                wide = product(held[k, at], mine[...])
                for m in range(per // 2):
                    for q in range(nz * nc):
                        for n in range(2):
                            e = 2 * m + n
                            part[q % nc, q // nc, base + h * per // 2 + m, 8 * n:8 * n + 8] = (
                                wide[8 * q:8 * q + 8, e * BLK:(e + 1) * BLK]
                            )

            lo, hi = base + h * per // 2, base + (h + 1) * per // 2
            moving = reduce(step, lo, hi)
            step += 1
            for move in waiting:
                finish(*move)
            waiting = [(moving, lo, hi)]
    for move in waiting:
        finish(*move)
    if split:
        shares = [total[base + i] for i in range(per)]

        @pl.when(wrap == 0)
        def _():
            for e in range(per):
                n, m = e % 2, e // 2
                total[base + e] = jnp.concatenate(
                    [shares[m][:, n * half:(n + 1) * half], shares[per // 2 + m][:, n * half:(n + 1) * half]],
                    axis=1,
                )

        @pl.when(wrap != 0)
        def _():
            for e in range(per):
                n, m = e % 2, e // 2
                total[base + e] = jnp.concatenate(
                    [shares[m][8 * n:8 * n + 8], shares[per // 2 + m][8 * n:8 * n + 8]], axis=0
                )

        give.wait()
    for copy in pending:
        copy.wait_send()

    for table in tables[1:]:
        table.wait()
    first_slots = nb * per * (nb * per - 1) // 2
    live = count_ref[b]
    for p in range(pmax):
        u = first_ref[b, p]
        v = second_ref[b, p]
        u = lax.rem(u // per - b + nb, nb) * per + lax.rem(u, per)
        v = lax.rem(v // per - b + nb, nb) * per + lax.rem(v, per)
        big = jnp.maximum(u, v)
        small = jnp.minimum(u, v)
        value = total[jnp.minimum(big * (big - 1) // 2 + small, first_slots - 1)]
        out_ref[p] = jnp.where(p < live, value, jnp.zeros_like(value))


def shards(mesh, integrals, need_blocks, pair_first, pair_second, pair_count):
    nb, nz, nc = mesh.shape["basis"], mesh.shape["aux"], mesh.shape["occ"]
    size, aux_size, occ_size = integrals.shape
    local = size // BLK
    width = aux_size * occ_size
    pmax = pair_first.shape[1]
    blocks = need_blocks.shape[1]
    per = blocks // nb
    slots = blocks * (blocks - 1) // 2
    rows = BLK // (nz * nc)
    split = nb == 2 and per == 4 and rows == 16
    slots += per - 1 if split else 0
    steps = 3 + blocks - per
    x = integrals.reshape(local, BLK, aux_size, occ_size)
    f32, bf16 = jnp.float32, jnp.bfloat16
    out = pl.pallas_call(
        functools.partial(kernel, nb, nz, nc, per, split),
        out_shape=jax.ShapeDtypeStruct((pmax, rows, BLK), f32),
        in_specs=[pl.BlockSpec(memory_space=pltpu.HBM)] * 5,
        out_specs=pl.BlockSpec(memory_space=pltpu.VMEM),
        scratch_shapes=[
            *[
                pltpu.SMEM(table.shape, jnp.int32)
                for table in (need_blocks, pair_first, pair_second, pair_count)
            ],
            *[pltpu.VMEM((local, BLK // CUT, aux_size, occ_size), bf16)] * CUT,
            pltpu.VMEM((blocks - per, BLK, width), bf16),
            pltpu.VMEM((blocks - per, BLK, width), bf16),
            pltpu.VMEM((per * BLK, width), bf16),
            pltpu.VMEM((nc, nz, slots, rows, BLK), f32),
            pltpu.VMEM((nc - 1, nz, slots, rows, BLK), f32),
            pltpu.VMEM((nz, slots, rows, BLK), f32),
            pltpu.VMEM((nz - 1, slots, rows, BLK), f32),
            pltpu.VMEM((slots, rows, BLK), f32),
            pltpu.VMEM((BLK, width), bf16),
            pltpu.SemaphoreType.DMA((CUT,)),
            pltpu.SemaphoreType.DMA((4,)),
            pltpu.SemaphoreType.DMA((blocks - per, CUT)),
            pltpu.SemaphoreType.DMA((blocks - per, CUT)),
            pltpu.SemaphoreType.DMA((steps, nc - 1)),
            pltpu.SemaphoreType.DMA((steps, nc - 1)),
            pltpu.SemaphoreType.DMA((steps, nz - 1)),
            pltpu.SemaphoreType.DMA((steps, nz - 1)),
            pltpu.SemaphoreType.DMA,
            pltpu.SemaphoreType.DMA,
        ],
        compiler_params=pltpu.CompilerParams(
            collective_id=0, has_side_effects=True, vmem_limit_bytes=61 * 2**20
        ),
    )(need_blocks, pair_first, pair_second, pair_count, x)
    return out[None]


def solution(mesh):
    in_specs = (
        P(("groups", "basis"), "aux", "occ"),
        P("groups", None),
        P("groups", None),
        P("groups", None),
        P("groups"),
    )
    out_specs = P(("groups", "basis"), None, ("aux", "occ"), None)
    return jax.shard_map(
        functools.partial(shards, mesh), mesh=mesh, in_specs=in_specs, out_specs=out_specs, check_vma=False
    )
```

```python
import functools

import jax
import jax.numpy as jnp
from jax import lax
from jax.experimental import pallas as pl
from jax.experimental.pallas import tpu as pltpu
from jax.sharding import PartitionSpec as P

BLK = 128
CUT = 4
MESH = pl.DeviceIdType.MESH


def kernel(
    nb, nz, nc, per, split,
    need_in, first_in, second_in, count_in, x_ref,
    out_ref,
    need_ref, first_ref, second_ref, count_ref, *rest,
):
    xv, rest = rest[:CUT], rest[CUT:]
    sent, held, mine, part, other, summed, come, total, spare = rest[:9]
    load_sem, arg_sem, x_send, x_recv, c_send, c_recv, z_send, z_recv, g_send, g_recv = rest[9:]
    b = lax.axis_index("basis")
    z = lax.axis_index("aux")
    c = lax.axis_index("occ")
    local = x_ref.shape[0]
    piece = BLK // CUT
    rows = part.shape[3]
    pmax = out_ref.shape[0]

    tables = []
    for i, (src, dst) in enumerate((
        (need_in, need_ref), (first_in, first_ref), (second_in, second_ref), (count_in, count_ref)
    )):
        table = pltpu.make_async_copy(src, dst, arg_sem.at[i])
        table.start()
        tables.append(table)
    loads = []
    for i in range(CUT):
        load = pltpu.make_async_copy(x_ref.at[:, pl.ds(i * piece, piece)], xv[i], load_sem.at[i])
        load.start()
        loads.append(load)

    x_peers = [lax.rem(b + s, nb) for s in range(1, nb)]
    z_peers = [lax.rem(z + o, nz) for o in range(1, nz)]
    c_peers = [lax.rem(c + o, nc) for o in range(1, nc)]
    barrier = pltpu.get_barrier_semaphore()
    for d in x_peers:
        pl.semaphore_signal(barrier, inc=1, device_id={"basis": d}, device_id_type=MESH)
    for d in z_peers:
        pl.semaphore_signal(barrier, inc=1, device_id={"aux": d}, device_id_type=MESH)
    for d in c_peers:
        pl.semaphore_signal(barrier, inc=1, device_id={"occ": d}, device_id_type=MESH)
    tables[0].wait()
    pl.semaphore_wait(barrier, len(x_peers) + len(z_peers) + len(c_peers))

    def pack(owner, j, i, dst):
        block = lax.rem(need_ref[owner, b * per + j], local)
        dst[...] = xv[i][block].reshape(piece, dst.shape[1])

    def pack_strided(owner, j, i, dst):
        block = lax.rem(need_ref[owner, b * per + j], local)
        h, quarter = i // 2, i % 2
        taken = []
        for n in range(4):
            row = 16 * (4 * quarter + n) + 8 * h
            taken.append(xv[row // piece][block, row % piece:row % piece + 8])
        dst[...] = jnp.concatenate(taken, axis=0).reshape(piece, dst.shape[1])

    pending = []
    for s in range(1, nb):
        d = lax.rem(b + nb - s, nb)
        for j in range(per):
            k = (s - 1) * per + j
            for i in range(CUT):
                at = pl.ds(i * piece, piece)
                if len(pending) < CUT:
                    loads[i].wait()
                if split and k == per - 1:
                    @pl.when(d == 0)
                    def _():
                        pack(d, j, i, sent.at[k, at])

                    @pl.when(d != 0)
                    def _():
                        pack_strided(d, j, i, sent.at[k, at])

                    pack(d, j, i, spare.at[at])
                else:
                    pack(d, j, i, sent.at[k, at])
                copy = pltpu.make_async_remote_copy(
                    src_ref=sent.at[k, at],
                    dst_ref=held.at[k, at],
                    send_sem=x_send.at[k, i],
                    recv_sem=x_recv.at[k, i],
                    device_id={"basis": d},
                    device_id_type=MESH,
                )
                pending.append(copy)
                if len(pending) <= CUT:
                    copy.start()
    for j in range(per):
        for i in range(CUT):
            pack(b, j, i, mine.at[pl.ds(j * BLK + i * piece, piece)])

    def put(tile, slot):
        for q in range(nz * nc):
            part[q % nc, q // nc, slot] = tile[q * rows:(q + 1) * rows, :]

    def product(lhs, rhs):
        return lax.dot_general(
            lhs, rhs, (((1,), (1,)), ((), ())), preferred_element_type=jnp.float32
        )

    def exchange(step, lo, hi):
        copies = []
        for o, d in enumerate(c_peers):
            copy = pltpu.make_async_remote_copy(
                src_ref=part.at[d, :, lo:hi],
                dst_ref=other.at[o, :, lo:hi],
                send_sem=c_send.at[step, o],
                recv_sem=c_recv.at[step, o],
                device_id={"occ": d},
                device_id_type=MESH,
            )
            copy.start()
            copies.append(copy)
        return copies

    def spread(step, lo, hi):
        for slot in range(lo, hi):
            for q in range(nz):
                value = part[c, q, slot]
                for o in range(len(c_peers)):
                    value = value + other[o, q, slot]
                summed[q, slot] = value
        copies = []
        for o, d in enumerate(z_peers):
            copy = pltpu.make_async_remote_copy(
                src_ref=summed.at[d, lo:hi],
                dst_ref=come.at[o, lo:hi],
                send_sem=z_send.at[step, o],
                recv_sem=z_recv.at[step, o],
                device_id={"aux": d},
                device_id_type=MESH,
            )
            copy.start()
            copies.append(copy)
        return copies

    def finish(copies, lo, hi):
        for copy in copies:
            copy.wait()
        for slot in range(lo, hi):
            value = summed[z, slot]
            for o in range(len(z_peers)):
                value = value + come[o, slot]
            total[slot] = value

    def reduce(step, lo, hi):
        copies = exchange(step, lo, hi)
        for copy in copies:
            copy.wait()
        return spread(step, lo, hi)

    def own(j):
        return mine[j * BLK:(j + 1) * BLK, :]

    for a in range(1, per):
        for e in range(a):
            put(product(own(e), own(a)), a * (a - 1) // 2 + e)
    landed = [0]

    def pump(upto):
        for i in range(landed[0], upto):
            pending[i].wait_recv()
            if i + CUT < len(pending):
                pending[i + CUT].start()
        landed[0] = max(landed[0], upto)

    lo, hi = 0, per * (per - 1) // 2
    waiting = [(reduce(0, lo, hi), lo, hi)]
    step = 1
    give = None
    if split:
        pump(2)
        base = total.shape[0] - (per - 1)
        for e in range(per - 1):
            put(product(sent[e], spare[...]), base + e)
        waiting.append((reduce(step, base, base + per - 1), base, base + per - 1))
        step += 1
        give = pltpu.make_async_remote_copy(
            src_ref=total.at[base:base + per - 1],
            dst_ref=total.at[base - (per - 1):base],
            send_sem=g_send,
            recv_sem=g_recv,
            device_id={"basis": x_peers[0]},
            device_id_type=MESH,
        )
    for a in range(per, nb * per):
        k = a - per
        s = a // per
        wrap = (b + s) // nb
        base = a * (a - 1) // 2
        if split and a == nb * per - 1:
            break
        pump((k + 1) * CUT)

        @pl.when(wrap == 0)
        def _():
            wide = product(mine[...], held[k])
            for e in range(per):
                put(wide[e * BLK:(e + 1) * BLK, :], base + e)

        @pl.when(wrap != 0)
        def _():
            wide = product(held[k], mine[...])
            for e in range(per):
                put(wide[:, e * BLK:(e + 1) * BLK], base + e)

        for e in range(per, a):
            flip = wrap - (b + e // per) // nb
            first = (e - per) + flip * (a - e)
            second = k - flip * (a - e)
            put(product(held[first], held[second]), base + e)
        lo, hi = base, base + a
        moving = reduce(step, lo, hi)
        step += 1
        for move in waiting:
            finish(*move)
        waiting = [(moving, lo, hi)]
        if split and a == per:
            give.start()
    if split:
        half = BLK // 2
        for h in range(2):
            pump(k * CUT + 2 * h + 2)
            at = slice(h * half, (h + 1) * half)

            @pl.when(wrap == 0)
            def _():
                wide = product(mine[...], held[k, at])
                for m in range(per // 2):
                    left = wide[2 * m * BLK:(2 * m + 1) * BLK, :]
                    right = wide[(2 * m + 1) * BLK:(2 * m + 2) * BLK, :]
                    put(jnp.concatenate([left, right], axis=1), base + h * per // 2 + m)

            @pl.when(wrap != 0)
            def _():
                wide = product(held[k, at], mine[...])
                for m in range(per // 2):
                    for q in range(nz * nc):
                        for n in range(2):
                            e = 2 * m + n
                            part[q % nc, q // nc, base + h * per // 2 + m, 8 * n:8 * n + 8] = (
                                wide[8 * q:8 * q + 8, e * BLK:(e + 1) * BLK]
                            )

            lo, hi = base + h * per // 2, base + (h + 1) * per // 2
            moving = reduce(step, lo, hi)
            step += 1
            for move in waiting:
                finish(*move)
            waiting = [(moving, lo, hi)]
    for move in waiting:
        finish(*move)
    if split:
        shares = [total[base + i] for i in range(per)]

        @pl.when(wrap == 0)
        def _():
            for e in range(per):
                n, m = e % 2, e // 2
                total[base + e] = jnp.concatenate(
                    [shares[m][:, n * half:(n + 1) * half], shares[per // 2 + m][:, n * half:(n + 1) * half]],
                    axis=1,
                )

        @pl.when(wrap != 0)
        def _():
            for e in range(per):
                n, m = e % 2, e // 2
                total[base + e] = jnp.concatenate(
                    [shares[m][8 * n:8 * n + 8], shares[per // 2 + m][8 * n:8 * n + 8]], axis=0
                )

        give.wait()
    for copy in pending:
        copy.wait_send()

    for table in tables[1:]:
        table.wait()
    first_slots = nb * per * (nb * per - 1) // 2
    live = count_ref[b]
    for p in range(pmax):
        u = first_ref[b, p]
        v = second_ref[b, p]
        u = lax.rem(u // per - b + nb, nb) * per + lax.rem(u, per)
        v = lax.rem(v // per - b + nb, nb) * per + lax.rem(v, per)
        big = jnp.maximum(u, v)
        small = jnp.minimum(u, v)
        value = total[jnp.minimum(big * (big - 1) // 2 + small, first_slots - 1)]
        out_ref[p] = jnp.where(p < live, value, jnp.zeros_like(value))


def shards(mesh, integrals, need_blocks, pair_first, pair_second, pair_count):
    nb, nz, nc = mesh.shape["basis"], mesh.shape["aux"], mesh.shape["occ"]
    size, aux_size, occ_size = integrals.shape
    local = size // BLK
    width = aux_size * occ_size
    pmax = pair_first.shape[1]
    blocks = need_blocks.shape[1]
    per = blocks // nb
    slots = blocks * (blocks - 1) // 2
    rows = BLK // (nz * nc)
    split = nb == 2 and per == 4 and rows == 16
    slots += per - 1 if split else 0
    steps = 3 + blocks - per
    x = integrals.reshape(local, BLK, aux_size, occ_size)
    f32, bf16 = jnp.float32, jnp.bfloat16
    out = pl.pallas_call(
        functools.partial(kernel, nb, nz, nc, per, split),
        out_shape=jax.ShapeDtypeStruct((pmax, rows, BLK), f32),
        in_specs=[pl.BlockSpec(memory_space=pltpu.HBM)] * 5,
        out_specs=pl.BlockSpec(memory_space=pltpu.VMEM),
        scratch_shapes=[
            *[
                pltpu.SMEM(table.shape, jnp.int32)
                for table in (need_blocks, pair_first, pair_second, pair_count)
            ],
            *[pltpu.VMEM((local, BLK // CUT, aux_size, occ_size), bf16)] * CUT,
            pltpu.VMEM((blocks - per, BLK, width), bf16),
            pltpu.VMEM((blocks - per, BLK, width), bf16),
            pltpu.VMEM((per * BLK, width), bf16),
            pltpu.VMEM((nc, nz, slots, rows, BLK), f32),
            pltpu.VMEM((nc - 1, nz, slots, rows, BLK), f32),
            pltpu.VMEM((nz, slots, rows, BLK), f32),
            pltpu.VMEM((nz - 1, slots, rows, BLK), f32),
            pltpu.VMEM((slots, rows, BLK), f32),
            pltpu.VMEM((BLK, width), bf16),
            pltpu.SemaphoreType.DMA((CUT,)),
            pltpu.SemaphoreType.DMA((4,)),
            pltpu.SemaphoreType.DMA((blocks - per, CUT)),
            pltpu.SemaphoreType.DMA((blocks - per, CUT)),
            pltpu.SemaphoreType.DMA((steps, nc - 1)),
            pltpu.SemaphoreType.DMA((steps, nc - 1)),
            pltpu.SemaphoreType.DMA((steps, nz - 1)),
            pltpu.SemaphoreType.DMA((steps, nz - 1)),
            pltpu.SemaphoreType.DMA,
            pltpu.SemaphoreType.DMA,
        ],
        compiler_params=pltpu.CompilerParams(
            collective_id=0, has_side_effects=True, vmem_limit_bytes=61 * 2**20
        ),
    )(need_blocks, pair_first, pair_second, pair_count, x)
    return out[None]


def solution(mesh):
    in_specs = (
        P(("groups", "basis"), "aux", "occ"),
        P("groups", None),
        P("groups", None),
        P("groups", None),
        P("groups"),
    )
    out_specs = P(("groups", "basis"), None, ("aux", "occ"), None)
    return jax.shard_map(
        functools.partial(shards, mesh), mesh=mesh, in_specs=in_specs, out_specs=out_specs, check_vma=False
    )
```
